512 devices in a mesh: net: 64 (over z, x), scen: 8 (over y, core).
Axes of the slice: x: 4, y: 4, z: 16, core: 2. Of those that a mesh axis runs over, the one named last changes fastest.
Arguments:
- device_group: int32 [64], replicated, may hold values from 3 to 63, as said below
- column_blocks: int32 [256, 12], P('net'), may hold values from 0 to 255, as said below
- impedance_real: bfloat16 [256, 12, 128, 128], P('net'), may hold values from 0 to 0.015258789
- impedance_imag: bfloat16 [256, 12, 128, 128], P('net'), may hold values from 0 to 0.0076293945
- building_phase: int32 [65536], P('net'), may hold values from 0 to 32767, as said below
- building_power: float32 [65536], P('net'), may hold values from 0.2 to 1
- reactive_ratio: float32 [65536], P('net'), may hold values from 0.1 to 0.8
- copula_normals: float32 [65536, 1024], P('net', 'scen'), may hold values from -6 to 6
- source_angle: float32 [32768], P('net'), may hold values from -3.140625 to 3.140625
Outputs:
- voltage_real: float32 [32768, 1024], P('net', 'scen')
- voltage_imag: float32 [32768, 1024], P('net', 'scen')
- drop_mean: float32 [32768, 16], P('net')
The draws below stay inside these ranges and needn't reach their ends.
Inputs may be any that keep to these rules, and one draw needn't show every extreme that they name: `device_group`: never falling along the devices; each group is a run of 1 to 4 consecutive devices and is labelled by the index of its last device; the first 4 devices form one group. `column_blocks`: slot 0 of block row r is r itself; the first min(12, 4 times the devices of r's group) slots are distinct blocks of devices of r's group; the other slots repeat r. `building_phase`: building b feeds a phase of the device that holds b: from 512 * (b // 1024) to that plus 512 - 1; every phase is fed by at least one building.
All inputs are finite; a program needn't handle non-finite values.
Results may differ from the reference program's by a relative error of at most 0.0063.
Values may be sent and summed in bfloat16 or wider, within the bound.
No kernel may reach another device: no remote copies, remote signals or barrier semaphores. Data moves between devices by JAX's collectives and lax.ppermute only.
A program may use at most 64 MiB of HBM per device.

```python
import math
import jax
import jax.numpy as jnp
from jax import lax

BP = 128
NNZ = 12
GMAX = 4
ITERS = 3
TIMES = 16
BLK_DEV = 4
PH_DEV = 512
BLD_DEV = 1024
BLOCKS = 256
PHASES = 32768
BUILDINGS = 65536
SCEN = 64
N_NET = 64


def feeder_groups(key):
    run_lengths = jax.random.randint(jax.random.fold_in(key, 11), (N_NET,), 1, GMAX + 1)
    run_lengths = run_lengths.at[0].set(GMAX)

    def advance(state_pair, unused):
        group_now, remain = state_pair
        starting = remain == 0
        group_now = jnp.where(starting, group_now + 1, group_now)
        fetched = run_lengths[jnp.clip(group_now, 0, N_NET - 1)]
        remain = jnp.where(starting, fetched, remain) - 1
        return ((group_now, remain), group_now)
    final_state, groups = lax.scan(advance, (jnp.int32(-1), jnp.int32(0)), None, length=N_NET)
    devices = jnp.arange(N_NET, dtype=jnp.int32)
    same_group = groups[:, None] == groups[None, :]
    last_device = jnp.max(jnp.where(same_group, devices[None, :], -1), axis=1)
    return last_device.astype(jnp.int32)


def draw_device_group(key, part):
    return feeder_groups(key)


def draw_column_blocks(key, part):
    groups = feeder_groups(key)
    devices = jnp.arange(N_NET, dtype=jnp.int32)
    same_group = groups[:, None] == groups[None, :]
    first_device = jnp.min(jnp.where(same_group, devices[None, :], N_NET), axis=1)
    group_size = jnp.sum(same_group.astype(jnp.int32), axis=1)
    rows_all = jnp.arange(BLOCKS, dtype=jnp.int32)
    owner = rows_all // BLK_DEV
    group_start = first_device[owner] * BLK_DEV
    group_blocks = group_size[owner] * BLK_DEV
    offsets = jnp.arange(GMAX * BLK_DEV, dtype=jnp.int32)
    candidate = group_start[:, None] + offsets[None, :]
    invalid = (offsets[None, :] >= group_blocks[:, None]) | (candidate == rows_all[:, None])
    scores = jax.random.randint(jax.random.fold_in(key, 13), (BLOCKS, GMAX * BLK_DEV), 0, 1 << 20) * (GMAX * BLK_DEV) + offsets[None, :]
    scores = jnp.where(invalid, 1 << 30, scores)
    order = jnp.argsort(scores, axis=1)[:, :NNZ - 1].astype(jnp.int32)
    picked = group_start[:, None] + order
    live_other = jnp.minimum(NNZ, group_blocks) - 1
    slots = jnp.arange(NNZ - 1, dtype=jnp.int32)
    picked = jnp.where(slots[None, :] < live_other[:, None], picked, rows_all[:, None])
    return jnp.concatenate([rows_all[:, None], picked], axis=1).astype(jnp.int32)


def draw_building_phase(key, part):
    device_keys = jax.random.split(jax.random.fold_in(key, 17), N_NET)
    orders = jax.vmap(lambda one_key: jax.random.permutation(one_key, BLD_DEV))(device_keys)
    extra = jax.random.randint(jax.random.fold_in(key, 19), (N_NET, BLD_DEV), 0, PH_DEV)
    local_phase = jnp.where(orders < PH_DEV, orders, extra)
    placed = local_phase + jnp.arange(N_NET, dtype=jnp.int32)[:, None] * PH_DEV
    return placed.reshape(-1).astype(jnp.int32)


def levels(stream_key, extent, shards, smallest, largest):
    level = 1.0
    for dim, shards_of in shards:
        draws = jax.random.uniform(jax.random.fold_in(jax.random.fold_in(stream_key, 6), dim), (shards_of,), jnp.float32, smallest / len(shards), largest / len(shards))
        level = level * jnp.repeat(jnp.exp(draws), extent[dim] // shards_of).reshape((-1,) + (1,) * (len(extent) - 1 - dim))
    return level


def normal_values(key, dims, scale, most, shards=(), kind=jnp.bfloat16):
    result = scale * jax.random.normal(key, dims, jnp.float32)
    if shards:
        result = result * levels(key, dims, shards, -0.22, 0.18)
    return jnp.clip(result, -most, most).astype(kind)


def setup_inputs(seed: int = 0) -> dict:
    streams_of = jax.random.split(jax.random.key(seed), 10)
    return {
        "device_group": draw_device_group(jax.random.fold_in(streams_of[9], 71), 0),
        "column_blocks": draw_column_blocks(jax.random.fold_in(streams_of[9], 71), 0),
        "impedance_real": jnp.clip(0.015258789 * jax.random.uniform(streams_of[2], (BLOCKS, NNZ, BP, BP), jnp.float32) ** levels(streams_of[2], (BLOCKS, NNZ, BP, BP), ((0, 64),), -0.2, 0.2), 0.0, 0.015258789).astype(jnp.bfloat16),
        "impedance_imag": jnp.clip(0.0076293945 * jax.random.uniform(streams_of[3], (BLOCKS, NNZ, BP, BP), jnp.float32) ** levels(streams_of[3], (BLOCKS, NNZ, BP, BP), ((0, 64),), -0.2, 0.2), 0.0, 0.0076293945).astype(jnp.bfloat16),
        "building_phase": draw_building_phase(jax.random.fold_in(streams_of[9], 71), 0),
        "building_power": jnp.clip(jnp.exp(math.log(1.0) - 1.609438 * jax.random.uniform(streams_of[5], (BUILDINGS,), jnp.float32) ** levels(streams_of[5], (BUILDINGS,), ((0, 64),), -0.2, 0.2)), 0.2, 1.0),
        "reactive_ratio": jnp.clip(0.1 + 0.7 * jax.random.uniform(streams_of[6], (BUILDINGS,), jnp.float32) ** levels(streams_of[6], (BUILDINGS,), ((0, 64),), -0.2, 0.2), 0.1, 0.8),
        "copula_normals": normal_values(streams_of[7], (BUILDINGS, SCEN * TIMES), 1.0, 6.0, ((0, 64), (1, 8)), jnp.float32),
        "source_angle": jnp.clip(jax.random.uniform(streams_of[8], (PHASES,), jnp.float32, -3.140625, 3.140625), -3.140625, 3.140625),
    }


floor_square = 0.49

def reference(device_group, column_blocks, impedance_real, impedance_imag, building_phase, building_power, reactive_ratio, copula_normals, source_angle):
    column_total = SCEN * TIMES
    scenario = (jnp.arange(column_total, dtype=jnp.int32) // TIMES).astype(jnp.float32)
    scen_level = 0.5 + scenario / (SCEN - 1)
    real_power = building_power[:, None] * scen_level[None, :] * jnp.exp(0.4 * copula_normals - 0.08)
    reactive = real_power * reactive_ratio[:, None]
    load_real = jax.ops.segment_sum(real_power, building_phase, num_segments=PHASES)
    load_reactive = jax.ops.segment_sum(reactive, building_phase, num_segments=PHASES)
    source_real = jnp.broadcast_to(jnp.cos(source_angle)[:, None], (PHASES, column_total))
    source_imag = jnp.broadcast_to(jnp.sin(source_angle)[:, None], (PHASES, column_total))
    same_group = device_group[:, None] == device_group[None, :]
    group_size = lax.optimization_barrier(jnp.sum(same_group.astype(jnp.int32), axis=1))
    live_count = jnp.minimum(NNZ, group_size * BLK_DEV)
    owner = jnp.arange(BLOCKS, dtype=jnp.int32) // BLK_DEV
    live_mask = (jnp.arange(NNZ, dtype=jnp.int32)[None, :] < live_count[owner][:, None]).astype(jnp.float32)
    volt_real = source_real
    volt_imag = source_imag
    for sweep in range(ITERS):
        mag_square = jnp.maximum(volt_real * volt_real + volt_imag * volt_imag, floor_square)
        current_real = (load_real * volt_real + load_reactive * volt_imag) / mag_square
        current_imag = (load_real * volt_imag - load_reactive * volt_real) / mag_square
        currents = jnp.concatenate([current_real, current_imag], axis=1).astype(jnp.bfloat16)
        current_blocks = currents.reshape(BLOCKS, BP, 2 * column_total)

        def block_row(row_args):
            row_real, row_imag, row_columns, row_live = row_args
            picked = current_blocks[row_columns].astype(jnp.float32) * row_live[:, None, None]
            real_part = jnp.einsum('sij,sjk->ik', row_real.astype(jnp.float32), picked, precision=lax.Precision.HIGHEST)
            imag_part = jnp.einsum('sij,sjk->ik', row_imag.astype(jnp.float32), picked, precision=lax.Precision.HIGHEST)
            return (real_part, imag_part)
        real_part, imag_part = lax.map(block_row, (impedance_real, impedance_imag, column_blocks, live_mask))
        real_part = real_part.reshape(PHASES, 2 * column_total)
        imag_part = imag_part.reshape(PHASES, 2 * column_total)
        drop_real = real_part[:, :column_total] - imag_part[:, column_total:]
        drop_imag = real_part[:, column_total:] + imag_part[:, :column_total]
        volt_real = source_real - drop_real
        volt_imag = source_imag - drop_imag
    magnitude = jnp.sqrt(volt_real * volt_real + volt_imag * volt_imag)
    drop_mean = 100.0 * (1.0 - lax.optimization_barrier(jnp.mean(magnitude.reshape(PHASES, SCEN, TIMES), axis=1)))
    return (volt_real, volt_imag, drop_mean)
```

```python
import functools

import jax
import jax.numpy as jnp
from jax import lax
from jax.experimental import pallas as pl
from jax.experimental.pallas import tpu as pltpu
from jax.sharding import PartitionSpec as P

GMAX = 4
ITERS = 3
TIMES = 16
FLOOR = 0.49
LANES = 128
VMEM_BYTES = 24 * 1024 * 1024
f32, bf16 = jnp.float32, jnp.bfloat16


def split3(value):
    high = value.astype(bf16)
    rest = value - high.astype(f32)
    middle = rest.astype(bf16)
    return high, middle, (rest - middle.astype(f32)).astype(bf16)


def currents_of(volt_real, volt_imag, load_real, load_reactive):
    inverse = 1.0 / jnp.maximum(volt_real * volt_real + volt_imag * volt_imag, FLOOR)
    current_real = (load_real * volt_real + load_reactive * volt_imag) * inverse
    current_imag = (load_real * volt_imag - load_reactive * volt_real) * inverse
    return current_real.astype(bf16), current_imag.astype(bf16)


def front_kernel(where, group_ref, phase_ref, power_ref, ratio_ref, normals_ref, angle_ref,
                 place_ref, current_ref, load_real_ref, load_reactive_ref, source_real_ref, source_imag_ref, *, net_count, scen_total):
    net_index, scen_index = where[0], where[1]
    own = group_ref[net_index]
    before = jnp.int32(0)
    for distance in range(1, GMAX):
        other = group_ref[jnp.maximum(net_index - distance, 0)]
        before += ((net_index >= distance) & (other == own)).astype(jnp.int32)
    size = own - (net_index - before) + 1
    start = net_index - before
    place_ref[0] = jnp.where(size == 1, 0, jnp.where(size == 2, 1 + start % 2, jnp.where(size == 3, 3 + start % 3, 6 + start % 4)))
    place_ref[1] = start
    place_ref[2] = before

    blocks = phase_ref.shape[0]
    angle = angle_ref[...]
    count = angle.shape[0]
    phase_count = count * LANES
    stacked = jnp.concatenate(
        [power_ref[...], ratio_ref[...], jnp.cos(angle), jnp.sin(angle), jnp.zeros((LANES - 2 * blocks - 2 * count, LANES), f32)], axis=0)
    columns = stacked.T

    def column(k):
        return jnp.broadcast_to(columns[:, k:k + 1], (LANES, LANES))

    lane = lax.broadcasted_iota(jnp.int32, (1, LANES), 1)
    scenario = (scen_index * (LANES // TIMES) + lane // TIMES).astype(f32)
    level = 0.5 + scenario / (scen_total - 1)
    row = lax.broadcasted_iota(jnp.int32, (phase_count, LANES), 0) + net_index * phase_count
    hot, pieces = [], []
    for k in range(blocks):
        hot.append(jnp.where(row == phase_ref[k:k + 1, :], 1.0, 0.0).astype(bf16))
        part = normals_ref[k * LANES:(k + 1) * LANES, :]
        real_power = column(k) * level * jnp.exp(0.4 * part - 0.08)
        pieces.append(split3(jnp.concatenate([real_power, real_power * column(blocks + k)], axis=1)))
    hot = jnp.concatenate(hot, axis=1)
    loads = None
    for piece in zip(*pieces):
        term = jnp.dot(hot, jnp.concatenate(piece, axis=0), preferred_element_type=f32)
        loads = term if loads is None else loads + term
    load_real_ref[...] = loads[:, :LANES]
    load_reactive_ref[...] = loads[:, LANES:]
    for k in range(count):
        rows = slice(k * LANES, (k + 1) * LANES)
        source_real = column(2 * blocks + k)
        source_imag = column(2 * blocks + count + k)
        source_real_ref[rows, :] = source_real
        source_imag_ref[rows, :] = source_imag
        current_real, current_imag = currents_of(source_real, source_imag, loads[rows, :LANES], loads[rows, LANES:])
        for copy in range(GMAX):
            current_ref[copy, rows, :LANES] = current_real
            current_ref[copy, rows, LANES:] = current_imag


def front(where, group, phase, power, ratio, normals, angle, net_count, scen_total):
    building_count, columns = normals.shape
    phase_count = angle.shape[0]
    smem, vmem = pl.BlockSpec(memory_space=pltpu.SMEM), pl.BlockSpec(memory_space=pltpu.VMEM)
    return pl.pallas_call(
        functools.partial(front_kernel, net_count=net_count, scen_total=scen_total),
        out_shape=[jax.ShapeDtypeStruct((4,), jnp.int32), jax.ShapeDtypeStruct((GMAX, phase_count, 2 * columns), bf16)]
        + [jax.ShapeDtypeStruct((phase_count, columns), f32)] * 4,
        in_specs=[smem, smem] + [vmem] * 5,
        out_specs=[smem] + [vmem] * 5,
        compiler_params=pltpu.CompilerParams(vmem_limit_bytes=VMEM_BYTES),
        name="front",
    )(where, group, phase.reshape(-1, LANES), power.reshape(-1, LANES), ratio.reshape(-1, LANES), normals, angle.reshape(-1, LANES))


def sweep_kernel(place_ref, column_ref, impedance_real_ref, impedance_imag_ref, load_real_ref, load_reactive_ref,
                 source_real_ref, source_imag_ref, *refs, size, last):
    parts = 1 if size == GMAX else size
    window_refs, refs = refs[:parts], refs[parts:]
    block_count, slot_count, block_width, _ = impedance_real_ref.shape
    live = min(slot_count, size * block_count)
    if parts > 1:
        window_ref, outs = refs[-1], refs[:-1]
        for k in range(parts):
            window_ref[k * block_count:(k + 1) * block_count] = window_refs[k][...].reshape(block_count, block_width, -1)
    else:
        window_ref, outs = window_refs[0], refs
    start, before = place_ref[1], place_ref[2]
    if last:
        pick_lane = lax.broadcasted_iota(jnp.int32, (TIMES, LANES), 1)
        pick_row = lax.broadcasted_iota(jnp.int32, (TIMES, LANES), 0)
        pick = jnp.where(pick_lane % TIMES == pick_row, 1.0, 0.0).astype(bf16)
    for r in range(block_count):
        left_real, left_imag, right = [], [], []
        for s in range(live):
            member = column_ref[r, s] - start * block_count
            if size < GMAX:
                away = before - member // block_count
                away = jnp.where(away < 0, away + size, away)
                member = away * block_count + member % block_count
            left_real.append(impedance_real_ref[r, s])
            left_imag.append(impedance_imag_ref[r, s])
            right.append(window_ref[member])
        left = jnp.concatenate([jnp.concatenate(left_real, axis=1), jnp.concatenate(left_imag, axis=1)], axis=0)
        product = jnp.dot(left, jnp.concatenate(right, axis=0), preferred_element_type=f32)
        drop_real = product[:block_width, :LANES] - product[block_width:, LANES:]
        drop_imag = product[:block_width, LANES:] + product[block_width:, :LANES]
        rows = slice(r * block_width, (r + 1) * block_width)
        volt_real = source_real_ref[rows, :] - drop_real
        volt_imag = source_imag_ref[rows, :] - drop_imag
        if last:
            outs[0][rows, :] = volt_real
            outs[1][rows, :] = volt_imag
            magnitude = jnp.sqrt(volt_real * volt_real + volt_imag * volt_imag)
            total = None
            for piece in split3(magnitude):
                term = lax.dot_general(pick, piece, (((1,), (1,)), ((), ())), preferred_element_type=f32)
                total = term if total is None else total + term
            for copy in range(outs[2].shape[0]):
                outs[2][copy, :, rows] = total
        else:
            current_real, current_imag = currents_of(volt_real, volt_imag, load_real_ref[rows, :], load_reactive_ref[rows, :])
            if size == GMAX:
                for copy in range(GMAX):
                    outs[0][copy, rows, :LANES] = current_real
                    outs[0][copy, rows, LANES:] = current_imag
            else:
                outs[0][rows, :LANES] = current_real
                outs[0][rows, LANES:] = current_imag


def sweep(place, column_blocks, impedance_real, impedance_imag, loads, windows, size, last, scen_count):
    phase_count, columns = loads[0].shape
    block_count, _, block_width, _ = impedance_real.shape
    smem, vmem = pl.BlockSpec(memory_space=pltpu.SMEM), pl.BlockSpec(memory_space=pltpu.VMEM)
    if last:
        shapes = [jax.ShapeDtypeStruct((phase_count, columns), f32)] * 2 + [jax.ShapeDtypeStruct((scen_count, TIMES, phase_count), f32)]
    else:
        shapes = [jax.ShapeDtypeStruct(((GMAX,) if size == GMAX else ()) + (phase_count, 2 * columns), bf16)]
    scratch = [] if len(windows) == 1 else [pltpu.VMEM((len(windows) * block_count, block_width, 2 * columns), bf16)]
    if size == GMAX or size == 1:
        windows = [windows[0].reshape(size * block_count, block_width, 2 * columns)]
    return pl.pallas_call(
        functools.partial(sweep_kernel, size=size, last=last),
        out_shape=shapes,
        in_specs=[smem, smem] + [vmem] * (6 + len(windows)),
        out_specs=[vmem] * len(shapes),
        scratch_shapes=scratch,
        compiler_params=pltpu.CompilerParams(vmem_limit_bytes=VMEM_BYTES),
        name="sweep",
    )(place, column_blocks, impedance_real, impedance_imag, *loads, *windows)


def branch_of(size, offset, net_count, scen_count):
    starts = range(offset, net_count - size + 1, size)
    rings = [[(s + a, s + (a + turn) % size) for s in starts for a in range(size)] for turn in range(1, size)]
    quads = [[(s + offset + a) % net_count for a in range(GMAX)] for s in range(0, net_count, GMAX)]

    def exchange(current):
        if size == GMAX:
            return [lax.all_to_all(current, "net", 0, 0, axis_index_groups=quads)]
        return [current] + [lax.ppermute(current, "net", pairs) for pairs in rings]

    def run(current, place, column_blocks, impedance_real, impedance_imag, loads):
        if size < GMAX:
            current = current[0]
        for turn in range(ITERS):
            made = sweep(place, column_blocks, impedance_real, impedance_imag, loads, exchange(current), size, turn == ITERS - 1, scen_count)
            current = made[0]
        return tuple(made)

    return run


def finish_kernel(sums_ref, out_ref, *, scen_total):
    total = sums_ref[0]
    for k in range(1, sums_ref.shape[0]):
        total = total + sums_ref[k]
    out_ref[...] = (100.0 * (1.0 - total / scen_total)).T


def shards(device_group, column_blocks, impedance_real, impedance_imag, building_phase, building_power, reactive_ratio, copula_normals, source_angle):
    net_count, scen_count = lax.axis_size("net"), lax.axis_size("scen")
    column_count = copula_normals.shape[1]
    scen_total = column_count // TIMES * scen_count
    where = jnp.stack([lax.axis_index("net"), lax.axis_index("scen")]).astype(jnp.int32)
    place, current, *loads = front(
        where, device_group, building_phase, building_power, reactive_ratio, copula_normals, source_angle, net_count, scen_total)
    kinds = [(1, 0)] + [(size, offset) for size in range(2, GMAX + 1) for offset in range(size)]
    volt_real, volt_imag, sums = lax.switch(
        place[0], [branch_of(size, offset, net_count, scen_count) for size, offset in kinds],
        current, place, column_blocks, impedance_real, impedance_imag, loads)
    sums = lax.all_to_all(sums, "scen", 0, 0)
    phase_count = volt_real.shape[0]
    drop_mean = pl.pallas_call(
        functools.partial(finish_kernel, scen_total=scen_total),
        out_shape=jax.ShapeDtypeStruct((phase_count, TIMES), f32),
        in_specs=[pl.BlockSpec(memory_space=pltpu.VMEM)],
        out_specs=pl.BlockSpec(memory_space=pltpu.VMEM),
        name="finish",
    )(sums)
    return volt_real, volt_imag, drop_mean


def solution(mesh):
    in_specs = (P(), P("net", None), P("net", None, None, None), P("net", None, None, None), P("net"), P("net"), P("net"), P("net", "scen"), P("net"))
    out_specs = (P("net", "scen"), P("net", "scen"), P("net", None))
    return jax.shard_map(shards, mesh=mesh, in_specs=in_specs, out_specs=out_specs, check_vma=False)
```

```python
import functools

import jax
import jax.numpy as jnp
from jax import lax
from jax.experimental import pallas as pl
from jax.experimental.pallas import tpu as pltpu
from jax.sharding import PartitionSpec as P

GMAX = 4
ITERS = 3
TIMES = 16
FLOOR = 0.49
LANES = 128
VMEM_BYTES = 14 * 1024 * 1024
f32, bf16 = jnp.float32, jnp.bfloat16


def split3(value):
    high = value.astype(bf16)
    rest = value - high.astype(f32)
    middle = rest.astype(bf16)
    return high, middle, (rest - middle.astype(f32)).astype(bf16)


def currents_of(volt_real, volt_imag, load_real, load_reactive):
    inverse = 1.0 / jnp.maximum(volt_real * volt_real + volt_imag * volt_imag, FLOOR)
    current_real = (load_real * volt_real + load_reactive * volt_imag) * inverse
    current_imag = (load_real * volt_imag - load_reactive * volt_real) * inverse
    return current_real.astype(bf16), current_imag.astype(bf16)


def front_kernel(group_any, column_any, phase_any, power_any, ratio_any, normals_any, angle_any,
                 place_ref, current_ref, load_real_ref, load_reactive_ref, columns_ref,
                 group_ref, column_ref, phase_ref, power_ref, ratio_ref, normals_ref, angle_ref, sems, normal_sems, *, scen_total):
    pairs = [(angle_any, angle_ref), (power_any, power_ref), (ratio_any, ratio_ref), (phase_any, phase_ref), (group_any, group_ref), (column_any, column_ref)]
    copies = [pltpu.make_async_copy(source, target, sems.at[k]) for k, (source, target) in enumerate(pairs)]
    blocks = phase_ref.shape[0]
    chunks = [pltpu.make_async_copy(normals_any.at[pl.ds(k * LANES, LANES)], normals_ref.at[pl.ds(k * LANES, LANES)], normal_sems.at[k]) for k in range(blocks)]
    for copy in copies + chunks:
        copy.start()
    net_index, scen_index = lax.axis_index("net"), lax.axis_index("scen")
    for copy in copies + chunks:
        copy.wait()
    angle = angle_ref[...]
    count = angle.shape[0]
    phase_count = count * LANES
    stacked = jnp.concatenate(
        [jnp.cos(angle), jnp.sin(angle), power_ref[...], ratio_ref[...], jnp.zeros((LANES - 2 * blocks - 2 * count, LANES), f32)], axis=0)
    columns = stacked.T
    columns_ref[...] = columns

    def column(k):
        return jnp.broadcast_to(columns[:, k:k + 1], (LANES, LANES))

    lane = lax.broadcasted_iota(jnp.int32, (1, LANES), 1)
    scenario = (scen_index * (LANES // TIMES) + lane // TIMES).astype(f32)
    level = 0.5 + scenario / (scen_total - 1)
    row = lax.broadcasted_iota(jnp.int32, (phase_count, LANES), 0) + net_index * phase_count
    hot = jnp.concatenate([jnp.where(row == phase_ref[k:k + 1, :], 1.0, 0.0).astype(bf16) for k in range(blocks)], axis=1)

    own = group_ref[net_index]
    before = jnp.int32(0)
    for distance in range(1, GMAX):
        other = group_ref[jnp.maximum(net_index - distance, 0)]
        before += ((net_index >= distance) & (other == own)).astype(jnp.int32)
    start = net_index - before
    size = own - start + 1
    block_count, slot_count = column_ref.shape
    place_ref[0] = jnp.where(size == 1, 0, jnp.where(size == 2, 1 + start % 2, jnp.where(size == 3, 3 + start % 3, 6 + start % 4)))
    for r in range(block_count):
        for s in range(slot_count):
            member = column_ref[r, s] - start * block_count
            device = member // block_count
            away = before - device
            away = jnp.where(away < 0, away + size, away)
            device = jnp.where(size < GMAX, away, device)
            place_ref[1 + r * slot_count + s] = device * block_count + member % block_count

    pieces = []
    for k in range(blocks):
        part = normals_ref[k * LANES:(k + 1) * LANES, :]
        real_power = column(2 * count + k) * level * jnp.exp(0.4 * part - 0.08)
        pieces.append(split3(jnp.concatenate([real_power, real_power * column(2 * count + blocks + k)], axis=1)))
    loads = None
    for piece in zip(*pieces):
        term = jnp.dot(hot, jnp.concatenate(piece, axis=0), preferred_element_type=f32)
        loads = term if loads is None else loads + term
    load_real_ref[...] = loads[:, :LANES]
    load_reactive_ref[...] = loads[:, LANES:]
    for k in range(count):
        rows = slice(k * LANES, (k + 1) * LANES)
        source_real = column(k)
        source_imag = column(count + k)
        current_real, current_imag = currents_of(source_real, source_imag, loads[rows, :LANES], loads[rows, LANES:])
        for copy in range(GMAX):
            current_ref[copy, rows, :LANES] = current_real
            current_ref[copy, rows, LANES:] = current_imag


def front(group, column_blocks, phase, power, ratio, normals, angle, scen_total):
    building_count, columns = normals.shape
    phase_count = angle.shape[0]
    smem, vmem = pl.BlockSpec(memory_space=pltpu.SMEM), pl.BlockSpec(memory_space=pltpu.VMEM)
    packed = [x.reshape(-1, LANES) for x in (phase, power, ratio)]
    angle = angle.reshape(-1, LANES)
    return pl.pallas_call(
        functools.partial(front_kernel, scen_total=scen_total),
        out_shape=[jax.ShapeDtypeStruct((1 + column_blocks.size,), jnp.int32), jax.ShapeDtypeStruct((GMAX, phase_count, 2 * columns), bf16)]
        + [jax.ShapeDtypeStruct((phase_count, columns), f32)] * 2 + [jax.ShapeDtypeStruct((LANES, LANES), f32)],
        in_specs=[pl.BlockSpec(memory_space=pltpu.HBM)] * 7,
        out_specs=[smem] + [vmem] * 4,
        scratch_shapes=[pltpu.SMEM(group.shape, jnp.int32), pltpu.SMEM(column_blocks.shape, jnp.int32)]
        + [pltpu.VMEM(x.shape, x.dtype) for x in (*packed, normals, angle)]
        + [pltpu.SemaphoreType.DMA((6,)), pltpu.SemaphoreType.DMA((building_count // LANES,))],
        compiler_params=pltpu.CompilerParams(vmem_limit_bytes=VMEM_BYTES),
        name="front",
    )(*[pltpu.with_memory_space_constraint(x, pltpu.HBM) for x in (group, column_blocks, *packed, normals, angle)])


def sweep_kernel(place_ref, impedance_real_ref, impedance_imag_ref, load_real_ref, load_reactive_ref, columns_ref, *refs, size, last):
    parts = 1 if size == GMAX else size
    window_refs, refs = refs[:parts], list(refs[parts:])
    block_count, slot_count, block_width, _ = impedance_real_ref.shape
    live = min(slot_count, size * block_count)
    window_ref = window_refs[0]
    if parts > 1:
        window_ref = refs.pop()
        for k in range(parts):
            window_ref[k * block_count:(k + 1) * block_count] = window_refs[k][...].reshape(block_count, block_width, -1)
    copies = []
    for r in range(block_count):
        left_real, left_imag, right = [], [], []
        for s in range(live):
            left_real.append(impedance_real_ref[r, s])
            left_imag.append(impedance_imag_ref[r, s])
            right.append(window_ref[place_ref[1 + r * slot_count + s]])
        left = jnp.concatenate([jnp.concatenate(left_real, axis=1), jnp.concatenate(left_imag, axis=1)], axis=0)
        product = jnp.dot(left, jnp.concatenate(right, axis=0), preferred_element_type=f32)
        drop_real = product[:block_width, :LANES] - product[block_width:, LANES:]
        drop_imag = product[:block_width, LANES:] + product[block_width:, :LANES]
        rows = slice(r * block_width, (r + 1) * block_width)
        volt_real = jnp.broadcast_to(columns_ref[:, r:r + 1], (block_width, LANES)) - drop_real
        volt_imag = jnp.broadcast_to(columns_ref[:, block_count + r:block_count + r + 1], (block_width, LANES)) - drop_imag
        if last:
            volt_real_any, volt_imag_any, sums_ref, volt_ref, sems = refs
            volt_ref[0, rows, :] = volt_real
            volt_ref[1, rows, :] = volt_imag
            for k, target in enumerate((volt_real_any, volt_imag_any)):
                span = pl.ds(r * block_width, block_width)
                copies.append(pltpu.make_async_copy(volt_ref.at[k, span], target.at[span], sems.at[k, r]))
                copies[-1].start()
            turned = jnp.sqrt(volt_real * volt_real + volt_imag * volt_imag).T
            total = turned[:TIMES]
            for s in range(1, LANES // TIMES):
                total = total + turned[s * TIMES:(s + 1) * TIMES]
            for copy in range(sums_ref.shape[0]):
                sums_ref[copy, :, rows] = total
        else:
            current_real, current_imag = currents_of(volt_real, volt_imag, load_real_ref[rows, :], load_reactive_ref[rows, :])
            for copy in range(GMAX if size == GMAX else 1):
                refs[0][copy, rows, :LANES] = current_real
                refs[0][copy, rows, LANES:] = current_imag
    for copy in copies:
        copy.wait()


def sweep(place, impedance_real, impedance_imag, loads, windows, size, last, scen_count):
    phase_count, columns = loads[0].shape
    block_count, _, block_width, _ = impedance_real.shape
    smem, vmem = pl.BlockSpec(memory_space=pltpu.SMEM), pl.BlockSpec(memory_space=pltpu.VMEM)
    scratch = []
    if last:
        shapes = [jax.ShapeDtypeStruct((phase_count, columns), f32)] * 2 + [jax.ShapeDtypeStruct((scen_count, TIMES, phase_count), f32)]
        out_specs = [pl.BlockSpec(memory_space=pltpu.HBM)] * 2 + [vmem]
        scratch = [pltpu.VMEM((2, phase_count, columns), f32), pltpu.SemaphoreType.DMA((2, block_count))]
    else:
        shapes = [jax.ShapeDtypeStruct((GMAX if size == GMAX else 1, phase_count, 2 * columns), bf16)]
        out_specs = [vmem]
    if len(windows) > 1:
        scratch.append(pltpu.VMEM((len(windows) * block_count, block_width, 2 * columns), bf16))
    else:
        windows = [windows[0].reshape(size * block_count, block_width, 2 * columns)]
    return pl.pallas_call(
        functools.partial(sweep_kernel, size=size, last=last),
        out_shape=shapes,
        in_specs=[smem] + [vmem] * (5 + len(windows)),
        out_specs=out_specs,
        scratch_shapes=scratch,
        compiler_params=pltpu.CompilerParams(vmem_limit_bytes=VMEM_BYTES),
        name="sweep",
    )(place, impedance_real, impedance_imag, *loads, *windows)


def branch_of(size, offset, net_count, scen_count):
    starts = range(offset, net_count - size + 1, size)
    rings = [[(s + a, s + (a + turn) % size) for s in starts for a in range(size)] for turn in range(1, size)]
    quads = [[(s + offset + a) % net_count for a in range(GMAX)] for s in range(0, net_count, GMAX)]

    def exchange(current):
        if size == GMAX:
            return [lax.all_to_all(current, "net", 0, 0, axis_index_groups=quads)]
        return [current] + [lax.ppermute(current, "net", pairs) for pairs in rings]

    def run(current, place, impedance_real, impedance_imag, loads):
        if size < GMAX:
            current = current[:1]
        for turn in range(ITERS):
            made = sweep(place, impedance_real, impedance_imag, loads, exchange(current), size, turn == ITERS - 1, scen_count)
            current = made[0]
        return tuple(made)

    return run


def shards(device_group, column_blocks, impedance_real, impedance_imag, building_phase, building_power, reactive_ratio, copula_normals, source_angle):
    net_count, scen_count = lax.axis_size("net"), lax.axis_size("scen")
    column_count = copula_normals.shape[1]
    scen_total = column_count // TIMES * scen_count
    place, current, *loads = front(
        device_group, column_blocks, building_phase, building_power, reactive_ratio, copula_normals, source_angle, scen_total)
    kinds = [(1, 0)] + [(size, offset) for size in range(2, GMAX + 1) for offset in range(size)]
    volt_real, volt_imag, sums = lax.switch(
        place[0], [branch_of(size, offset, net_count, scen_count) for size, offset in kinds],
        current, place, impedance_real, impedance_imag, loads)
    sums = lax.all_to_all(sums, "scen", 0, 0)
    drop_mean = 100.0 * (1.0 - jnp.sum(sums, axis=0) / scen_total)
    return volt_real, volt_imag, drop_mean.T


def solution(mesh):
    in_specs = (P(), P("net", None), P("net", None, None, None), P("net", None, None, None), P("net"), P("net"), P("net"), P("net", "scen"), P("net"))
    out_specs = (P("net", "scen"), P("net", "scen"), P("net", None))
    return jax.shard_map(shards, mesh=mesh, in_specs=in_specs, out_specs=out_specs, check_vma=False)
```

```python
import functools

import jax
import jax.numpy as jnp
from jax import lax
from jax.experimental import pallas as pl
from jax.experimental.pallas import tpu as pltpu
from jax.sharding import PartitionSpec as P

GMAX = 4
ITERS = 3
TIMES = 16
FLOOR = 0.49
LANES = 128
VMEM_BYTES = 7 * 1024 * 1024
f32, bf16 = jnp.float32, jnp.bfloat16


def split2(value):
    high = value.astype(bf16)
    return high, (value - high.astype(f32)).astype(bf16)


def currents_of(volt_real, volt_imag, load_real, load_reactive):
    inverse = 1.0 / jnp.maximum(volt_real * volt_real + volt_imag * volt_imag, FLOOR)
    current_real = (load_real * volt_real + load_reactive * volt_imag) * inverse
    current_imag = (load_real * volt_imag - load_reactive * volt_real) * inverse
    return current_real.astype(bf16), current_imag.astype(bf16)


def front_kernel(group_any, column_any, phase_any, power_any, ratio_any, normals_any, angle_any, impedance_real_any, impedance_imag_any,
                 place_ref, current_ref, load_real_ref, load_reactive_ref, columns_ref, impedance_real_ref, impedance_imag_ref,
                 group_ref, column_ref, phase_ref, power_ref, ratio_ref, normals_ref, angle_ref, sems, normal_sems, *, scen_total):
    pairs = [(angle_any, angle_ref), (power_any, power_ref), (ratio_any, ratio_ref), (phase_any, phase_ref), (group_any, group_ref), (column_any, column_ref),
             (impedance_real_any, impedance_real_ref), (impedance_imag_any, impedance_imag_ref)]
    copies = [pltpu.make_async_copy(source, target, sems.at[k]) for k, (source, target) in enumerate(pairs)]
    blocks = phase_ref.shape[0]
    chunks = [pltpu.make_async_copy(normals_any.at[pl.ds(k * LANES, LANES)], normals_ref.at[pl.ds(k * LANES, LANES)], normal_sems.at[k]) for k in range(blocks)]
    for copy in copies[:6] + chunks + copies[6:]:
        copy.start()
    net_index, scen_index = lax.axis_index("net"), lax.axis_index("scen")
    for copy in copies[:6] + chunks:
        copy.wait()
    angle = angle_ref[...]
    count = angle.shape[0]
    phase_count = count * LANES
    stacked = jnp.concatenate(
        [jnp.cos(angle), jnp.sin(angle), power_ref[...], ratio_ref[...], jnp.zeros((LANES - 2 * blocks - 2 * count, LANES), f32)], axis=0)
    columns = stacked.T
    columns_ref[...] = columns

    def column(k):
        return jnp.broadcast_to(columns[:, k:k + 1], (LANES, LANES))

    lane = lax.broadcasted_iota(jnp.int32, (1, LANES), 1)
    scenario = (scen_index * (LANES // TIMES) + lane // TIMES).astype(f32)
    level = 0.5 + scenario / (scen_total - 1)
    row = lax.broadcasted_iota(jnp.int32, (phase_count, LANES), 0) + net_index * phase_count
    hot = jnp.concatenate([jnp.where(row == phase_ref[k:k + 1, :], 1.0, 0.0).astype(bf16) for k in range(blocks)], axis=1)

    own = group_ref[net_index]
    before = jnp.int32(0)
    for distance in range(1, GMAX):
        other = group_ref[jnp.maximum(net_index - distance, 0)]
        before += ((net_index >= distance) & (other == own)).astype(jnp.int32)
    start = net_index - before
    size = own - start + 1
    block_count, slot_count = column_ref.shape
    place_ref[0] = jnp.where(size == 1, 0, jnp.where(size == 2, 1 + start % 2, jnp.where(size == 3, 3 + start % 3, 6 + start % 4)))
    for r in range(block_count):
        for s in range(slot_count):
            member = column_ref[r, s] - start * block_count
            device = member // block_count
            away = before - device
            away = jnp.where(away < 0, away + size, away)
            device = jnp.where(size < GMAX, away, device)
            place_ref[1 + r * slot_count + s] = device * block_count + member % block_count

    pieces = []
    for k in range(blocks):
        part = normals_ref[k * LANES:(k + 1) * LANES, :]
        real_power = column(2 * count + k) * level * jnp.exp(0.4 * part - 0.08)
        pieces.append(split2(jnp.concatenate([real_power, real_power * column(2 * count + blocks + k)], axis=1)))
    loads = None
    for piece in zip(*pieces):
        term = jnp.dot(hot, jnp.concatenate(piece, axis=0), preferred_element_type=f32)
        loads = term if loads is None else loads + term
    load_real_ref[...] = loads[:, :LANES]
    load_reactive_ref[...] = loads[:, LANES:]
    for k in range(count):
        rows = slice(k * LANES, (k + 1) * LANES)
        source_real = column(k)
        source_imag = column(count + k)
        current_real, current_imag = currents_of(source_real, source_imag, loads[rows, :LANES], loads[rows, LANES:])
        for copy in range(GMAX):
            current_ref[copy, rows, :LANES] = current_real
            current_ref[copy, rows, LANES:] = current_imag
    for copy in copies[6:]:
        copy.wait()


def front(group, column_blocks, phase, power, ratio, normals, angle, impedance_real, impedance_imag, scen_total):
    building_count, columns = normals.shape
    phase_count = angle.shape[0]
    smem, vmem = pl.BlockSpec(memory_space=pltpu.SMEM), pl.BlockSpec(memory_space=pltpu.VMEM)
    packed = [x.reshape(-1, LANES) for x in (phase, power, ratio)]
    angle = angle.reshape(-1, LANES)
    return pl.pallas_call(
        functools.partial(front_kernel, scen_total=scen_total),
        out_shape=[jax.ShapeDtypeStruct((1 + column_blocks.size,), jnp.int32), jax.ShapeDtypeStruct((GMAX, phase_count, 2 * columns), bf16)]
        + [jax.ShapeDtypeStruct((phase_count, columns), f32)] * 2 + [jax.ShapeDtypeStruct((LANES, LANES), f32)]
        + [jax.ShapeDtypeStruct(x.shape, x.dtype) for x in (impedance_real, impedance_imag)],
        in_specs=[pl.BlockSpec(memory_space=pltpu.HBM)] * 9,
        out_specs=[smem] + [vmem] * 6,
        scratch_shapes=[pltpu.SMEM(group.shape, jnp.int32), pltpu.SMEM(column_blocks.shape, jnp.int32)]
        + [pltpu.VMEM(x.shape, x.dtype) for x in (*packed, normals, angle)]
        + [pltpu.SemaphoreType.DMA((8,)), pltpu.SemaphoreType.DMA((building_count // LANES,))],
        compiler_params=pltpu.CompilerParams(vmem_limit_bytes=VMEM_BYTES),
        name="front",
    )(*[pltpu.with_memory_space_constraint(x, pltpu.HBM) for x in (group, column_blocks, *packed, normals, angle, impedance_real, impedance_imag)])


def sweep_kernel(place_ref, impedance_real_ref, impedance_imag_ref, load_real_ref, load_reactive_ref, columns_ref, *refs, size, last):
    parts = 1 if size == GMAX else size
    window_refs, refs = refs[:parts], list(refs[parts:])
    block_count, slot_count, block_width, _ = impedance_real_ref.shape
    live = min(slot_count, size * block_count)
    window_ref = window_refs[0]
    if parts > 1:
        window_ref = refs.pop()
        for k in range(parts):
            window_ref[k * block_count:(k + 1) * block_count] = window_refs[k][...].reshape(block_count, block_width, -1)
    copies = []
    for r in range(block_count):
        left_real, left_imag, right = [], [], []
        for s in range(live):
            left_real.append(impedance_real_ref[r, s])
            left_imag.append(impedance_imag_ref[r, s])
            right.append(window_ref[place_ref[1 + r * slot_count + s]])
        left = jnp.concatenate([jnp.concatenate(left_real, axis=1), jnp.concatenate(left_imag, axis=1)], axis=0)
        product = jnp.dot(left, jnp.concatenate(right, axis=0), preferred_element_type=f32)
        drop_real = product[:block_width, :LANES] - product[block_width:, LANES:]
        drop_imag = product[:block_width, LANES:] + product[block_width:, :LANES]
        rows = slice(r * block_width, (r + 1) * block_width)
        volt_real = jnp.broadcast_to(columns_ref[:, r:r + 1], (block_width, LANES)) - drop_real
        volt_imag = jnp.broadcast_to(columns_ref[:, block_count + r:block_count + r + 1], (block_width, LANES)) - drop_imag
        if last:
            volt_real_any, volt_imag_any, sums_ref, volt_ref, sems = refs
            volt_ref[0, rows, :] = volt_real
            volt_ref[1, rows, :] = volt_imag
            for k, target in enumerate((volt_real_any, volt_imag_any)):
                span = pl.ds(r * block_width, block_width)
                copies.append(pltpu.make_async_copy(volt_ref.at[k, span], target.at[span], sems.at[k, r]))
                copies[-1].start()
            turned = jnp.sqrt(volt_real * volt_real + volt_imag * volt_imag).T
            total = turned[:TIMES]
            for s in range(1, LANES // TIMES):
                total = total + turned[s * TIMES:(s + 1) * TIMES]
            for copy in range(sums_ref.shape[0]):
                sums_ref[copy, :, rows] = total
        else:
            current_real, current_imag = currents_of(volt_real, volt_imag, load_real_ref[rows, :], load_reactive_ref[rows, :])
            for copy in range(GMAX if size == GMAX else 1):
                refs[0][copy, rows, :LANES] = current_real
                refs[0][copy, rows, LANES:] = current_imag
    for copy in copies:
        copy.wait()


def sweep(place, impedance_real, impedance_imag, loads, windows, size, last, scen_count):
    phase_count, columns = loads[0].shape
    block_count, _, block_width, _ = impedance_real.shape
    smem, vmem = pl.BlockSpec(memory_space=pltpu.SMEM), pl.BlockSpec(memory_space=pltpu.VMEM)
    scratch = []
    if last:
        shapes = [jax.ShapeDtypeStruct((phase_count, columns), f32)] * 2 + [pltpu.VMEM((scen_count, TIMES, phase_count), f32)]
        out_specs = [pl.BlockSpec(memory_space=pltpu.HBM)] * 2 + [vmem]
        scratch = [pltpu.VMEM((2, phase_count, columns), f32), pltpu.SemaphoreType.DMA((2, block_count))]
    else:
        shapes = [jax.ShapeDtypeStruct((GMAX if size == GMAX else 1, phase_count, 2 * columns), bf16)]
        out_specs = [vmem]
    if len(windows) > 1:
        scratch.append(pltpu.VMEM((len(windows) * block_count, block_width, 2 * columns), bf16))
    else:
        windows = [windows[0].reshape(size * block_count, block_width, 2 * columns)]
    return pl.pallas_call(
        functools.partial(sweep_kernel, size=size, last=last),
        out_shape=shapes,
        in_specs=[smem] + [vmem] * (5 + len(windows)),
        out_specs=out_specs,
        scratch_shapes=scratch,
        compiler_params=pltpu.CompilerParams(vmem_limit_bytes=VMEM_BYTES),
        name="sweep",
    )(place, impedance_real, impedance_imag, *loads, *windows)


def branch_of(size, offset, net_count, scen_count):
    starts = range(offset, net_count - size + 1, size)
    rings = [[(s + a, s + (a + turn) % size) for s in starts for a in range(size)] for turn in range(1, size)]
    quads = [[(s + offset + a) % net_count for a in range(GMAX)] for s in range(0, net_count, GMAX)]

    def exchange(current):
        if size == GMAX:
            return [lax.all_to_all(current, "net", 0, 0, axis_index_groups=quads)]
        return [current] + [lax.ppermute(current, "net", pairs) for pairs in rings]

    def run(current, place, impedance_real, impedance_imag, loads):
        if size < GMAX:
            current = current[:1]
        for turn in range(ITERS):
            made = sweep(place, impedance_real, impedance_imag, loads, exchange(current), size, turn == ITERS - 1, scen_count)
            current = made[0]
        return tuple(made)

    return run


def shards(device_group, column_blocks, impedance_real, impedance_imag, building_phase, building_power, reactive_ratio, copula_normals, source_angle):
    net_count, scen_count = lax.axis_size("net"), lax.axis_size("scen")
    column_count = copula_normals.shape[1]
    scen_total = column_count // TIMES * scen_count
    place, current, *loads, impedance_real, impedance_imag = front(
        device_group, column_blocks, building_phase, building_power, reactive_ratio, copula_normals, source_angle, impedance_real, impedance_imag, scen_total)
    kinds = [(1, 0)] + [(size, offset) for size in range(2, GMAX + 1) for offset in range(size)]
    volt_real, volt_imag, sums = lax.switch(
        place[0], [branch_of(size, offset, net_count, scen_count) for size, offset in kinds],
        current, place, impedance_real, impedance_imag, loads)
    sums = lax.all_to_all(sums, "scen", 0, 0)
    drop_mean = 100.0 * (1.0 - jnp.sum(sums, axis=0) / scen_total)
    return volt_real, volt_imag, drop_mean.T


def solution(mesh):
    in_specs = (P(), P("net", None), P("net", None, None, None), P("net", None, None, None), P("net"), P("net"), P("net"), P("net", "scen"), P("net"))
    out_specs = (P("net", "scen"), P("net", "scen"), P("net", None))
    return jax.shard_map(shards, mesh=mesh, in_specs=in_specs, out_specs=out_specs, check_vma=False)
```

```python
import functools

import jax
import jax.numpy as jnp
from jax import lax
from jax.experimental import pallas as pl
from jax.experimental.pallas import tpu as pltpu
from jax.sharding import PartitionSpec as P

GMAX = 4
ITERS = 3
TIMES = 16
FLOOR = 0.49
LANES = 128
VMEM_BYTES = 7 * 1024 * 1024
f32, bf16 = jnp.float32, jnp.bfloat16


def split2(value):
    high = value.astype(bf16)
    return high, (value - high.astype(f32)).astype(bf16)


def currents_of(volt_real, volt_imag, load_real, load_reactive):
    inverse = 1.0 / jnp.maximum(volt_real * volt_real + volt_imag * volt_imag, FLOOR)
    current_real = (load_real * volt_real + load_reactive * volt_imag) * inverse
    current_imag = (load_real * volt_imag - load_reactive * volt_real) * inverse
    return current_real.astype(bf16), current_imag.astype(bf16)


def front_kernel(group_any, column_any, phase_any, power_any, ratio_any, normals_any, angle_any, impedance_real_any, impedance_imag_any,
                 place_ref, current_ref, load_real_ref, load_reactive_ref, columns_ref, impedance_real_ref, impedance_imag_ref,
                 group_ref, column_ref, phase_ref, power_ref, ratio_ref, normals_ref, angle_ref, sems, normal_sems, *, scen_total):
    pairs = [(angle_any, angle_ref), (power_any, power_ref), (ratio_any, ratio_ref), (phase_any, phase_ref), (group_any, group_ref), (column_any, column_ref),
             (impedance_real_any, impedance_real_ref), (impedance_imag_any, impedance_imag_ref)]
    copies = [pltpu.make_async_copy(source, target, sems.at[k]) for k, (source, target) in enumerate(pairs)]
    blocks = phase_ref.shape[0]
    chunks = [pltpu.make_async_copy(normals_any.at[pl.ds(k * LANES, LANES)], normals_ref.at[pl.ds(k * LANES, LANES)], normal_sems.at[k]) for k in range(blocks)]
    for copy in copies[:6] + chunks + copies[6:]:
        copy.start()
    net_index, scen_index = lax.axis_index("net"), lax.axis_index("scen")
    for copy in copies[:6] + chunks:
        copy.wait()
    angle = angle_ref[...]
    count = angle.shape[0]
    phase_count = count * LANES
    stacked = jnp.concatenate(
        [jnp.cos(angle), jnp.sin(angle), power_ref[...], ratio_ref[...], jnp.zeros((LANES - 2 * blocks - 2 * count, LANES), f32)], axis=0)
    columns = stacked.T
    columns_ref[...] = columns

    def column(k):
        return jnp.broadcast_to(columns[:, k:k + 1], (LANES, LANES))

    lane = lax.broadcasted_iota(jnp.int32, (1, LANES), 1)
    scenario = (scen_index * (LANES // TIMES) + lane // TIMES).astype(f32)
    level = 0.5 + scenario / (scen_total - 1)
    row = lax.broadcasted_iota(jnp.int32, (phase_count, LANES), 0) + net_index * phase_count
    hot = jnp.concatenate([jnp.where(row == phase_ref[k:k + 1, :], 1.0, 0.0).astype(bf16) for k in range(blocks)], axis=1)

    own = group_ref[net_index]
    before = jnp.int32(0)
    for distance in range(1, GMAX):
        other = group_ref[jnp.maximum(net_index - distance, 0)]
        before += ((net_index >= distance) & (other == own)).astype(jnp.int32)
    start = net_index - before
    size = own - start + 1
    block_count, slot_count = column_ref.shape
    place_ref[0] = jnp.where(size == 1, 0, jnp.where(size == 2, 1 + start % 2, jnp.where(size == 3, 3 + start % 3, 6 + start % 4)))
    for r in range(block_count):
        for s in range(slot_count):
            member = column_ref[r, s] - start * block_count
            device = member // block_count
            away = before - device
            away = jnp.where(away < 0, away + size, away)
            device = jnp.where(size < GMAX, away, device)
            place_ref[1 + r * slot_count + s] = device * block_count + member % block_count

    pieces = []
    for k in range(blocks):
        part = normals_ref[k * LANES:(k + 1) * LANES, :]
        real_power = column(2 * count + k) * level * jnp.exp(0.4 * part - 0.08)
        pieces.append(split2(jnp.concatenate([real_power, real_power * column(2 * count + blocks + k)], axis=1)))
    loads = None
    for piece in zip(*pieces):
        term = jnp.dot(hot, jnp.concatenate(piece, axis=0), preferred_element_type=f32)
        loads = term if loads is None else loads + term
    load_real_ref[...] = loads[:, :LANES]
    load_reactive_ref[...] = loads[:, LANES:]
    for k in range(count):
        rows = slice(k * LANES, (k + 1) * LANES)
        source_real = column(k)
        source_imag = column(count + k)
        current_real, current_imag = currents_of(source_real, source_imag, loads[rows, :LANES], loads[rows, LANES:])
        for copy in range(GMAX):
            current_ref[copy, rows, :LANES] = current_real
            current_ref[copy, rows, LANES:] = current_imag
    for copy in copies[6:]:
        copy.wait()


def front(group, column_blocks, phase, power, ratio, normals, angle, impedance_real, impedance_imag, scen_total):
    building_count, columns = normals.shape
    phase_count = angle.shape[0]
    smem, vmem = pl.BlockSpec(memory_space=pltpu.SMEM), pl.BlockSpec(memory_space=pltpu.VMEM)
    packed = [x.reshape(-1, LANES) for x in (phase, power, ratio)]
    angle = angle.reshape(-1, LANES)
    return pl.pallas_call(
        functools.partial(front_kernel, scen_total=scen_total),
        out_shape=[jax.ShapeDtypeStruct((1 + column_blocks.size,), jnp.int32), jax.ShapeDtypeStruct((GMAX, phase_count, 2 * columns), bf16)]
        + [jax.ShapeDtypeStruct((phase_count, columns), f32)] * 2 + [jax.ShapeDtypeStruct((LANES, LANES), f32)]
        + [jax.ShapeDtypeStruct(x.shape, x.dtype) for x in (impedance_real, impedance_imag)],
        in_specs=[pl.BlockSpec(memory_space=pltpu.HBM)] * 9,
        out_specs=[smem] + [vmem] * 6,
        scratch_shapes=[pltpu.SMEM(group.shape, jnp.int32), pltpu.SMEM(column_blocks.shape, jnp.int32)]
        + [pltpu.VMEM(x.shape, x.dtype) for x in (*packed, normals, angle)]
        + [pltpu.SemaphoreType.DMA((8,)), pltpu.SemaphoreType.DMA((building_count // LANES,))],
        compiler_params=pltpu.CompilerParams(vmem_limit_bytes=VMEM_BYTES),
        name="front",
    )(*[pltpu.with_memory_space_constraint(x, pltpu.HBM) for x in (group, column_blocks, *packed, normals, angle, impedance_real, impedance_imag)])


def sweep_kernel(place_ref, impedance_real_ref, impedance_imag_ref, load_real_ref, load_reactive_ref, columns_ref, *refs, size, last):
    parts = 1 if size == GMAX else size
    window_refs, refs = refs[:parts], list(refs[parts:])
    block_count, slot_count, block_width, _ = impedance_real_ref.shape
    live = min(slot_count, size * block_count)
    window_ref = window_refs[0]
    if parts > 1:
        window_ref = refs.pop()
        for k in range(parts):
            window_ref[k * block_count:(k + 1) * block_count] = window_refs[k][...].reshape(block_count, block_width, -1)
    for r in range(block_count):
        left_real, left_imag, right = [], [], []
        for s in range(live):
            left_real.append(impedance_real_ref[r, s])
            left_imag.append(impedance_imag_ref[r, s])
            right.append(window_ref[place_ref[1 + r * slot_count + s]])
        left = jnp.concatenate([jnp.concatenate(left_real, axis=1), jnp.concatenate(left_imag, axis=1)], axis=0)
        product = jnp.dot(left, jnp.concatenate(right, axis=0), preferred_element_type=f32)
        drop_real = product[:block_width, :LANES] - product[block_width:, LANES:]
        drop_imag = product[:block_width, LANES:] + product[block_width:, :LANES]
        rows = slice(r * block_width, (r + 1) * block_width)
        volt_real = jnp.broadcast_to(columns_ref[:, r:r + 1], (block_width, LANES)) - drop_real
        volt_imag = jnp.broadcast_to(columns_ref[:, block_count + r:block_count + r + 1], (block_width, LANES)) - drop_imag
        if last:
            volt_real_ref, volt_imag_ref, sums_ref = refs
            volt_real_ref[rows, :] = volt_real
            volt_imag_ref[rows, :] = volt_imag
            turned = jnp.sqrt(volt_real * volt_real + volt_imag * volt_imag).T
            total = turned[:TIMES]
            for s in range(1, LANES // TIMES):
                total = total + turned[s * TIMES:(s + 1) * TIMES]
            for copy in range(sums_ref.shape[0]):
                sums_ref[copy, :, rows] = total
        else:
            current_real, current_imag = currents_of(volt_real, volt_imag, load_real_ref[rows, :], load_reactive_ref[rows, :])
            for copy in range(GMAX if size == GMAX else 1):
                refs[0][copy, rows, :LANES] = current_real
                refs[0][copy, rows, LANES:] = current_imag


def sweep(place, impedance_real, impedance_imag, loads, windows, size, last, scen_count):
    phase_count, columns = loads[0].shape
    block_count, _, block_width, _ = impedance_real.shape
    smem, vmem = pl.BlockSpec(memory_space=pltpu.SMEM), pl.BlockSpec(memory_space=pltpu.VMEM)
    scratch = []
    if last:
        shapes = [pltpu.VMEM((phase_count, columns), f32)] * 2 + [pltpu.VMEM((scen_count, TIMES, phase_count), f32)]
        out_specs = [vmem] * 3
    else:
        shapes = [jax.ShapeDtypeStruct((GMAX if size == GMAX else 1, phase_count, 2 * columns), bf16)]
        out_specs = [vmem]
    if len(windows) > 1:
        scratch.append(pltpu.VMEM((len(windows) * block_count, block_width, 2 * columns), bf16))
    else:
        windows = [windows[0].reshape(size * block_count, block_width, 2 * columns)]
    return pl.pallas_call(
        functools.partial(sweep_kernel, size=size, last=last),
        out_shape=shapes,
        in_specs=[smem] + [vmem] * (5 + len(windows)),
        out_specs=out_specs,
        scratch_shapes=scratch,
        compiler_params=pltpu.CompilerParams(vmem_limit_bytes=VMEM_BYTES),
        name="sweep",
    )(place, impedance_real, impedance_imag, *loads, *windows)


def branch_of(size, offset, net_count, scen_count):
    starts = range(offset, net_count - size + 1, size)
    rings = [[(s + a, s + (a + turn) % size) for s in starts for a in range(size)] for turn in range(1, size)]
    quads = [[(s + offset + a) % net_count for a in range(GMAX)] for s in range(0, net_count, GMAX)]

    def exchange(current):
        if size == GMAX:
            return [lax.all_to_all(current, "net", 0, 0, axis_index_groups=quads)]
        return [current] + [lax.ppermute(current, "net", pairs) for pairs in rings]

    def run(current, place, impedance_real, impedance_imag, loads):
        if size < GMAX:
            current = current[:1]
        for turn in range(ITERS):
            made = sweep(place, impedance_real, impedance_imag, loads, exchange(current), size, turn == ITERS - 1, scen_count)
            current = made[0]
        return tuple(made)

    return run


def shards(device_group, column_blocks, impedance_real, impedance_imag, building_phase, building_power, reactive_ratio, copula_normals, source_angle):
    net_count, scen_count = lax.axis_size("net"), lax.axis_size("scen")
    column_count = copula_normals.shape[1]
    scen_total = column_count // TIMES * scen_count
    place, current, *loads, impedance_real, impedance_imag = front(
        device_group, column_blocks, building_phase, building_power, reactive_ratio, copula_normals, source_angle, impedance_real, impedance_imag, scen_total)
    kinds = [(1, 0)] + [(size, offset) for size in range(2, GMAX + 1) for offset in range(size)]
    volt_real, volt_imag, sums = lax.switch(
        place[0], [branch_of(size, offset, net_count, scen_count) for size, offset in kinds],
        current, place, impedance_real, impedance_imag, loads)
    sums = lax.all_to_all(sums, "scen", 0, 0)
    drop_mean = 100.0 * (1.0 - jnp.sum(sums, axis=0) / scen_total)
    return volt_real, volt_imag, drop_mean.T


def solution(mesh):
    in_specs = (P(), P("net", None), P("net", None, None, None), P("net", None, None, None), P("net"), P("net"), P("net"), P("net", "scen"), P("net"))
    out_specs = (P("net", "scen"), P("net", "scen"), P("net", None))
    return jax.shard_map(shards, mesh=mesh, in_specs=in_specs, out_specs=out_specs, check_vma=False)
```
